32 devices in a mesh: dp: 8 (over y, x, core), blk: 4 (over z).
Axes of the slice: x: 2, y: 2, z: 4, core: 2. Of those that a mesh axis runs over, the one named last changes fastest.
Arguments:
- layer_input: bfloat16 [4096, 2048], P(('dp', 'blk')), may hold values from -6 to 6
- out_grad: bfloat16 [4096, 2048], P(('dp', 'blk')), may hold values from -6 to 6
- expert_ids: int32 [4096, 2], P(('dp', 'blk')), may hold values from 0 to 7, all different within a row; in each aligned block of 128 rows (0 to 127, 128 to 255, ...) at most 40 rows name the same one
- combine: float32 [4096, 2], P(('dp', 'blk')), may hold values from 0.1 to 1
- bucket_ids: int32 [4096, 4], P(('dp', 'blk')), may hold values from 0 to 1023, as said below
- w_gate: bfloat16 [4, 8, 2048, 352], P('blk', 'dp'), may hold values from -0.125 to 0.125
- w_up: bfloat16 [4, 8, 2048, 352], P('blk', 'dp'), may hold values from -0.125 to 0.125
- w_down: bfloat16 [4, 8, 352, 2048], P('blk', 'dp'), may hold values from -0.15625 to 0.15625
Outputs:
- grad_gate: bfloat16 [4, 8, 2048, 352], P('blk', 'dp')
- grad_up: bfloat16 [4, 8, 2048, 352], P('blk', 'dp')
- grad_down: bfloat16 [4, 8, 352, 2048], P('blk', 'dp')
- ngram_grad: float32 [4, 1024, 2048], P(None, 'dp', 'blk')
The draws below stay inside these ranges and needn't reach their ends.
Inputs may be any that keep to these rules, and one draw needn't show every extreme that they name: `expert_ids`: within the 128 rows of one device (aligned blocks of rows) no expert is named more than 40 times. `bucket_ids`: within the 128 rows of one device (aligned blocks), at most 128 of the ids lie in any one range [128 * i, 128 * (i + 1)); on every device one such range, the same for all devices, holds exactly 128.
All inputs are finite; a program needn't handle non-finite values.
Results may differ from the reference program's by a relative error of at most 0.009.
Values may be sent and summed in bfloat16 or wider, within the bound.
A program may use at most 128 MiB of HBM per device.

```python
import math
import jax
import jax.numpy as jnp
import numpy as np
from jax import lax

D = 2048
FF = 1408
NHASH = 4
SHARDS = 4
TOK_DEV = 128
BUCK_DEV = 128
FF_DEV = 352
GROUPS = 4
QUADS = 2
EXPERTS = 8
CAP = 40
OWNCAP = 128
TOKENS = 4096
BUCKETS = 1024
N_DP = 8
N_BLK = 4


def draw_bucket_ids(key, part):
    block_total = TOKENS // TOK_DEV
    pair_total = TOK_DEV * NHASH
    owner_total = BUCKETS // BUCK_DEV
    ticket_total = owner_total * OWNCAP
    favored = jax.random.randint(jax.random.fold_in(key, 7), (), 0, owner_total)

    def one_block(number):
        block_key = jax.random.fold_in(key, 1000 + number)
        first_key, second_key, third_key, fourth_key = jax.random.split(block_key, 4)
        tickets = jnp.arange(ticket_total, dtype=jnp.int32)
        ticket_owner = tickets // OWNCAP
        priority = jax.random.permutation(first_key, ticket_total).astype(jnp.int32)
        priority = jnp.where(ticket_owner == favored, priority - ticket_total, priority)
        ordering = jnp.argsort(priority, stable=True)
        chosen = ticket_owner[ordering[:pair_total]]
        chosen = jax.random.permutation(second_key, chosen)
        limits = jax.random.randint(third_key, (pair_total,), 1, BUCK_DEV + 1)
        within = jax.random.randint(fourth_key, (pair_total,), 0, limits)
        return (chosen * BUCK_DEV + within).astype(jnp.int32).reshape(TOK_DEV, NHASH)
    blocks = jax.vmap(one_block)(jnp.arange(block_total, dtype=jnp.int32))
    return blocks.reshape(TOKENS, NHASH).astype(jnp.int32)


def shard_levels(rng, extent, pieces, low, largest):
    loudness, own = 1.0, jax.random.fold_in(rng, 6)
    for position, blocks in pieces:
        heights = jnp.exp(jax.random.uniform(jax.random.fold_in(own, position), (blocks,), jnp.float32, low / len(pieces), largest / len(pieces)))
        loudness = loudness * jnp.repeat(heights, extent[position] // blocks).reshape([-1 if axis == position else 1 for axis in range(len(extent))])
    return loudness


def deal_out(key, own, number, rows, amount, top, bound, lean):
    sequence = jax.random.permutation(key, amount)
    heavy_load, usual = load_shares(amount, rows * top, bound, lean, True), load_shares(amount, rows * top, bound, lean, False)
    places = jnp.arange(amount)

    def named(tallies, turn):
        used = int((tallies > 0).sum())
        fixed = max(1, used // 4)
        moved = fixed + (places - fixed + turn * (used - fixed)) % max(1, amount - fixed)
        return jnp.zeros((amount,), jnp.int32).at[sequence[jnp.where(places < fixed, places, moved)]].set(jnp.asarray(tallies, jnp.int32))

    tallies = jnp.where(number % 4 == 0, named(heavy_load, number // 4), named(usual, number - number // 4 - 1))
    mixed = jax.random.permutation(jax.random.fold_in(own, 3), amount)
    giver, sink = mixed[0:amount // 2 * 2:2], mixed[1:amount // 2 * 2:2]
    slack = jnp.minimum(tallies[giver] - 1, bound - tallies[sink]) // 2
    slack = jnp.where((giver == sequence[0]) | (sink == sequence[0]) | (tallies[sink] == 0), 0, jnp.maximum(slack, 0))
    moved = jax.random.randint(jax.random.fold_in(own, 4), (amount // 2,), 0, 1 << 20) % (slack + 1)
    tallies = tallies.at[giver].add(-moved).at[sink].add(moved)
    labels = jnp.searchsorted(jnp.cumsum(tallies), jnp.arange(rows * top), side="right").astype(jnp.int32)
    listing = labels.reshape(top, rows).T
    listing = listing[jax.random.permutation(jax.random.fold_in(own, 1), rows)]
    turn = jax.random.randint(jax.random.fold_in(own, 2), (rows, 1), 0, top)
    return jnp.take_along_axis(listing, (jnp.arange(top)[None, :] + turn) % top, axis=1)


def load_shares(count, total, limit, slope, full):
    weights = [(1 << 20) // math.isqrt(standing ** slope) + 1 for standing in range(1, count + 1)]
    largest = limit if full else min(limit, max(-(-total // count), total * weights[0] // sum(weights)))
    least = 1 if total - largest >= count - 1 else 0
    given, surplus = [largest] + [least] * (count - 1), total - largest - least * (count - 1)
    while surplus > 0:
        candidates = [i for i in range(1, count) if given[i] < largest] or [i for i in range(1, count) if given[i] < limit]
        mass, left = sum([weights[i] for i in candidates]), surplus
        for i in candidates:
            extra = min(limit - given[i], max(1, left * weights[i] // mass), surplus)
            given[i] = given[i] + extra
            surplus = surplus - extra
    return np.array(given)


def noise(rng, extent, spread, most, pieces=(), held_as=jnp.bfloat16):
    drawn = spread * jax.random.normal(rng, extent, jnp.float32)
    if pieces:
        drawn = drawn * shard_levels(rng, extent, pieces, -0.22, 0.18)
    return jnp.clip(drawn, -most, most).astype(held_as)


def setup_inputs(seed: int = 0) -> dict:
    seeds = jax.random.split(jax.random.key(seed), 9)
    layer_input = noise(seeds[0], (TOKENS, D), 1.0, 6.0, ((0, 32),))
    out_grad = noise(seeds[1], (TOKENS, D), 1.0, 6.0, ((0, 32),))
    expert_ids_keys = jax.random.split(jax.random.fold_in(seeds[2], 1), TOKENS // TOK_DEV)
    expert_ids_turns = jax.random.permutation(jax.random.fold_in(seeds[2], 3), TOKENS // TOK_DEV)
    expert_ids = jax.vmap(lambda own, number: deal_out(jax.random.fold_in(seeds[2], 2), own, number, TOK_DEV, EXPERTS, 2, CAP, 2))(expert_ids_keys, expert_ids_turns).reshape((TOKENS, 2))
    combine = jnp.clip(0.1 + 0.9 * jax.random.uniform(seeds[3], (TOKENS, 2), jnp.float32) ** shard_levels(seeds[3], (TOKENS, 2), ((0, 32),), -0.2, 0.2), 0.1, 1.0)
    bucket_ids = draw_bucket_ids(jax.random.fold_in(seeds[8], 71), 0)
    w_gate = noise(seeds[5], (GROUPS, QUADS * SHARDS, D, FF_DEV), D ** -0.5, 0.125, ((0, 4), (1, 8)))
    w_up = noise(seeds[6], (GROUPS, QUADS * SHARDS, D, FF_DEV), D ** -0.5, 0.125, ((0, 4), (1, 8)))
    w_down = noise(seeds[7], (GROUPS, QUADS * SHARDS, FF_DEV, D), FF ** -0.5, 0.15625, ((0, 4), (1, 8)))
    return dict(layer_input=layer_input, out_grad=out_grad, expert_ids=expert_ids, combine=combine, bucket_ids=bucket_ids, w_gate=w_gate, w_up=w_up, w_down=w_down)


def expert_block(rows_x, rows_g, gate_w, up_w, down_w):
    gate = jnp.dot(rows_x, gate_w, preferred_element_type=jnp.float32)
    upper = jnp.dot(rows_x, up_w, preferred_element_type=jnp.float32)
    sigma = jax.nn.sigmoid(gate)
    active = gate * sigma
    hidden = (active * upper).astype(jnp.bfloat16)
    d_hidden = lax.dot_general(rows_g, down_w, (((1,), (1,)), ((), ())), preferred_element_type=jnp.float32)
    d_up = (d_hidden * active).astype(jnp.bfloat16)
    d_gate = (d_hidden * upper * sigma * (1.0 + gate * (1.0 - sigma))).astype(jnp.bfloat16)
    d_rows = lax.dot_general(d_gate, gate_w, (((1,), (1,)), ((), ())), preferred_element_type=jnp.float32)
    d_rows = d_rows + lax.dot_general(d_up, up_w, (((1,), (1,)), ((), ())), preferred_element_type=jnp.float32)
    grad_down = lax.dot_general(hidden, rows_g, (((0,), (0,)), ((), ())), preferred_element_type=jnp.float32)
    grad_gate = lax.dot_general(rows_x, d_gate, (((0,), (0,)), ((), ())), preferred_element_type=jnp.float32)
    grad_up = lax.dot_general(rows_x, d_up, (((0,), (0,)), ((), ())), preferred_element_type=jnp.float32)
    return d_rows.astype(jnp.bfloat16), grad_gate, grad_up, grad_down


def reference(layer_input, out_grad, expert_ids, combine, bucket_ids, w_gate, w_up, w_down):
    token_total = layer_input.shape[0]
    pair_total = token_total * 2
    weighted = (combine[:, :, None] * out_grad[:, None, :].astype(jnp.float32)).astype(jnp.bfloat16)
    weighted = weighted.reshape(pair_total, D)
    expert_flat = expert_ids.reshape(pair_total).astype(jnp.int32)
    ordering = jnp.argsort(expert_flat, stable=True).astype(jnp.int32)
    counts = jnp.zeros((EXPERTS,), jnp.int32).at[expert_flat].add(1)
    starts = (jnp.cumsum(counts) - counts).astype(jnp.int32)
    most_rows = N_DP * N_BLK * CAP
    padded_order = jnp.concatenate([ordering, jnp.full((most_rows,), pair_total, jnp.int32)])
    gate_all = w_gate.reshape(EXPERTS, SHARDS, D, FF_DEV)
    up_all = w_up.reshape(EXPERTS, SHARDS, D, FF_DEV)
    down_all = w_down.reshape(EXPERTS, SHARDS, FF_DEV, D)

    def per_expert(slot_grads, expert):
        picks = lax.dynamic_slice_in_dim(padded_order, starts[expert], most_rows)
        inside = jnp.arange(most_rows, dtype=jnp.int32) < counts[expert]
        picks = jnp.where(inside, picks, pair_total).astype(jnp.int32)
        clipped = jnp.minimum(picks, pair_total - 1)
        rows_x = layer_input[clipped // 2]
        rows_g = jnp.where(inside[:, None], weighted[clipped], jnp.zeros((), weighted.dtype))
        summed = jnp.zeros((most_rows, D), jnp.float32)
        gate_parts, up_parts, down_parts = [], [], []
        for quarter in range(SHARDS):
            d_rows, grad_g, grad_u, grad_d = expert_block(rows_x, rows_g, gate_all[expert, quarter], up_all[expert, quarter], down_all[expert, quarter])
            summed = summed + d_rows.astype(jnp.float32)
            gate_parts.append(grad_g.astype(jnp.bfloat16))
            up_parts.append(grad_u.astype(jnp.bfloat16))
            down_parts.append(grad_d.astype(jnp.bfloat16))
        slot_grads = slot_grads.at[picks].set(summed.astype(jnp.bfloat16), mode="drop")
        return slot_grads, (jnp.stack(gate_parts), jnp.stack(up_parts), jnp.stack(down_parts))

    slot_init = jnp.zeros((pair_total, D), jnp.bfloat16)
    slot_grads, (grad_gate, grad_up, grad_down) = lax.scan(per_expert, slot_init, jnp.arange(EXPERTS, dtype=jnp.int32))
    slot_f = slot_grads.reshape(token_total, 2, D).astype(jnp.float32)
    emb_grad = (out_grad.astype(jnp.float32) + slot_f[:, 0] + slot_f[:, 1]).astype(jnp.bfloat16)
    emb_wide = emb_grad.astype(jnp.float32)
    tables = []
    for which in range(NHASH):
        tables.append(jnp.zeros((BUCKETS, D), jnp.float32).at[bucket_ids[:, which]].add(emb_wide))
    ngram_grad = jnp.stack(tables)
    grad_gate = grad_gate.reshape(N_BLK, N_DP, D, FF_DEV)
    grad_up = grad_up.reshape(N_BLK, N_DP, D, FF_DEV)
    grad_down = grad_down.reshape(N_BLK, N_DP, FF_DEV, D)
    return grad_gate, grad_up, grad_down, ngram_grad
```

```python
import jax
import jax.numpy as jnp
from jax import lax
from jax.sharding import Mesh, PartitionSpec as P

NHASH = 4
SHARDS = 4
BUCK_DEV = 128
F32 = jnp.float32
BF16 = jnp.bfloat16


def dot(a, b, ca, cb):
    return lax.dot_general(a, b, (((ca,), (cb,)), ((), ())), preferred_element_type=F32)


def slot_places(ids, quads, groups, capacity):
    tokens = ids.shape[0]
    expert_count = quads * groups
    dest = (ids % quads) * groups + ids // quads
    hot = (dest[:, :, None] == jnp.arange(expert_count)[None, None, :]).astype(F32)
    per_token = hot.sum(axis=1)
    before = jnp.tril(jnp.ones((tokens, tokens), F32), -1) @ per_token
    position = (hot * before[:, None, :]).sum(axis=2).astype(jnp.int32)
    return dest * capacity + position


def on_device(layer_input, out_grad, expert_ids, combine, bucket_ids, w_gate, w_up, w_down):
    groups = lax.axis_size("blk")
    quads = lax.axis_size("quad")
    experts = groups * quads
    tokens, width = layer_input.shape
    capacity = 5 * tokens // (2 * experts)
    piece = width // groups
    total = experts * capacity

    all_ids = lax.all_gather(expert_ids, "blk")
    all_buckets = lax.all_gather(bucket_ids, ("quad", "shard", "blk"), tiled=True)
    grad_pieces = lax.all_to_all(
        out_grad.reshape(tokens, groups, piece), "blk", split_axis=1, concat_axis=0, tiled=False
    ).reshape(groups, tokens, piece)

    slots = slot_places(expert_ids, quads, groups, capacity)
    number = jnp.arange(total, dtype=jnp.int32)[:, None]
    first = slots[:, 0][None, :] == number
    second = slots[:, 1][None, :] == number
    pick = (first | second).astype(BF16)
    scale = jnp.sum(
        jnp.where(first, combine[:, 0][None, :], 0.0)
        + jnp.where(second, combine[:, 1][None, :], 0.0),
        axis=1,
        keepdims=True,
    )
    send_x = dot(pick, layer_input, 1, 0).astype(BF16)
    send_w = (dot(pick, out_grad, 1, 0) * scale).astype(BF16)
    both = ("quad", "blk")
    rows_x = lax.all_to_all(send_x, both, split_axis=0, concat_axis=0, tiled=True)
    rows_w = lax.all_to_all(send_w, both, split_axis=0, concat_axis=0, tiled=True)
    rows_x = lax.all_gather(rows_x, "shard", tiled=True)
    rows_w = lax.all_gather(rows_w, "shard", tiled=True)

    gate_w, up_w, down_w = w_gate[0, 0], w_up[0, 0], w_down[0, 0]
    gate = dot(rows_x, gate_w, 1, 0)
    upper = dot(rows_x, up_w, 1, 0)
    sigma = jax.nn.sigmoid(gate)
    active = gate * sigma
    hidden = (active * upper).astype(BF16)
    d_hidden = dot(rows_w, down_w, 1, 1)
    d_up = (d_hidden * active).astype(BF16)
    d_gate = (d_hidden * upper * sigma * (1.0 + gate * (1.0 - sigma))).astype(BF16)
    part = (dot(d_gate, gate_w, 1, 1) + dot(d_up, up_w, 1, 1)).astype(BF16)
    grad_d = dot(hidden, rows_w, 0, 0).astype(BF16)
    grad_g = dot(rows_x, d_gate, 0, 0).astype(BF16)
    grad_u = dot(rows_x, d_up, 0, 0).astype(BF16)

    summed = lax.psum_scatter(part, "shard", scatter_dimension=0, tiled=True)
    outward = summed.reshape(quads, groups * capacity, groups, piece).transpose(0, 2, 1, 3)
    outward = outward.reshape(experts, groups * capacity, piece)
    back = lax.all_to_all(outward, both, split_axis=0, concat_axis=0, tiled=True)
    back = back.reshape(experts, groups, capacity, piece)

    embs = []
    for z in range(groups):
        places = slot_places(all_ids[z], quads, groups, capacity)
        put = (
            (places[:, 0][:, None] == number.T) | (places[:, 1][:, None] == number.T)
        ).astype(BF16)
        moved = dot(put, back[:, z].reshape(total, piece), 1, 0)
        embs.append((grad_pieces[z].astype(F32) + moved).astype(BF16))
    emb = jnp.concatenate(embs, axis=0)
    emb_all = lax.all_gather(emb, ("quad", "shard"), tiled=True)

    base = (lax.axis_index("quad") * SHARDS + lax.axis_index("shard")) * BUCK_DEV
    local = all_buckets - base
    hot = (local[:, :, None] == jnp.arange(BUCK_DEV)[None, None, :]).astype(BF16)
    hot = hot.reshape(all_buckets.shape[0], NHASH * BUCK_DEV)
    ngram = dot(hot, emb_all, 0, 0).reshape(NHASH, BUCK_DEV, piece)
    return grad_g[None, None], grad_u[None, None], grad_d[None, None], ngram


def solution(mesh):
    blocks = mesh.shape["blk"]
    quads = mesh.shape["dp"] // SHARDS
    split = Mesh(mesh.devices.reshape(quads, SHARDS, blocks), ("quad", "shard", "blk"))
    dp = ("quad", "shard")
    rows = P(dp + ("blk",), None)
    weights = P("blk", dp, None, None)
    return jax.shard_map(
        on_device,
        mesh=split,
        in_specs=(rows,) * 5 + (weights,) * 3,
        out_specs=(weights,) * 3 + (P(None, dp, "blk"),),
        check_vma=False,
    )
```

```python
import functools

import jax
import jax.numpy as jnp
from jax import lax
from jax.experimental import pallas as pl
from jax.experimental.pallas import tpu as pltpu
from jax.sharding import Mesh, PartitionSpec as P

NHASH = 4
SHARDS = 4
BUCK_DEV = 128
F32 = jnp.float32
BF16 = jnp.bfloat16


def dot(a, b, ca, cb):
    return lax.dot_general(a, b, (((ca,), (cb,)), ((), ())), preferred_element_type=F32)


def slot_places(ids, quads, groups, capacity):
    tokens = ids.shape[0]
    expert_count = quads * groups
    dest = (ids % quads) * groups + ids // quads
    hot = (dest[:, :, None] == jnp.arange(expert_count)[None, None, :]).astype(F32)
    per_token = hot.sum(axis=1)
    before = jnp.tril(jnp.ones((tokens, tokens), F32), -1) @ per_token
    position = (hot * before[:, None, :]).sum(axis=2).astype(jnp.int32)
    return dest * capacity + position


MESH = pl.DeviceIdType.MESH
SHARD = ("half", "core")


def place():
    return tuple(lax.axis_index(name) for name in ("quad", "half", "core", "blk"))


def greet(partners):
    barrier = pltpu.get_barrier_semaphore()
    for partner in partners:
        pl.semaphore_signal(barrier, inc=1, device_id=partner, device_id_type=MESH)
    pl.semaphore_wait(barrier, len(partners))


def remote(src, dst, sends, recvs, index, partner):
    return pltpu.make_async_remote_copy(
        src_ref=src,
        dst_ref=dst,
        send_sem=sends.at[index],
        recv_sem=recvs.at[index],
        device_id=partner,
        device_id_type=MESH,
    )


def return_kernel(
    quads, groups, part, grad, out, pieces, near, pair_sum, far, full, own_sem,
    sends1, recvs1, sends2, recvs2, sends3, recvs3, sends4, recvs4,
):
    q, x, c, z = place()
    rows, piece = full.shape[1], full.shape[2]
    quarter_rows = rows // quads
    others = [(k, j) for k in list(range(1, groups)) + [0] for j in range(quads) if k or j]
    order = list(range(1, groups)) + [0]

    def seat(k, j):
        return (lax.rem(q + j, quads), x, c, lax.rem(z + k, groups))

    other_core = (q, x, 1 - c, z)
    other_half = (q, 1 - x, c, z)
    greet([other_core, other_half] + [seat(k, j) for k, j in others])

    def block(k, j, core):
        half = lax.rem(x + 1 + j, 2)
        row = pl.multiple_of((half * 2 + core) * rows, 32)
        col = pl.multiple_of(lax.rem(z + k, groups) * piece, 128)
        return row, col

    def first(k, j):
        row, col = block(k, j, 1 - c)
        return remote(
            part.at[pl.ds(row, rows), pl.ds(col, piece)], near.at[j, k],
            sends1, recvs1, j * groups + k, other_core,
        )

    def second(k):
        return remote(pair_sum.at[k], far.at[k], sends2, recvs2, k, other_half)

    def third(k, j):
        start = pl.multiple_of(lax.rem(q + j, quads) * quarter_rows, 16)
        return remote(
            full.at[k, pl.ds(start, quarter_rows)], out.at[q * groups + z],
            sends3, recvs3, k * quads + j, seat(k, j),
        )

    def fourth(k):
        col = pl.multiple_of(lax.rem(z + k, groups) * piece, 128)
        return remote(
            grad.at[:, pl.ds(col, piece)], pieces.at[z], sends4, recvs4, k, seat(k, 0)
        )

    for j in range(2):
        for k in order:
            first(k, j).start()
    for k in range(1, groups):
        fourth(k).start()
    own_grad = pltpu.make_async_copy(
        grad.at[:, pl.ds(pl.multiple_of(z * piece, 128), piece)], pieces.at[z], own_sem.at[0]
    )
    own_grad.start()

    step = 32
    for k in order:
        first(k, 0).wait_recv()
        row, col = block(k, 0, c)

        @pl.loop(0, rows // step)
        def _(i):
            at = pl.multiple_of(i * step, step)
            mine = part[pl.ds(pl.multiple_of(row + at, step), step), pl.ds(col, piece)]
            theirs = near[0, k, pl.ds(at, step), :]
            pair_sum[k, pl.ds(at, step), :] = (mine.astype(F32) + theirs.astype(F32)).astype(BF16)

        second(k).start()
    for k in order:
        first(k, 1).wait_recv()
        second(k).wait_recv()
        row, col = block(k, 1, c)

        @pl.loop(0, rows // step)
        def _(i):
            at = pl.multiple_of(i * step, step)
            mine = part[pl.ds(pl.multiple_of(row + at, step), step), pl.ds(col, piece)]
            total = mine.astype(F32) + near[1, k, pl.ds(at, step), :].astype(F32)
            total = total + far[k, pl.ds(at, step), :].astype(F32)
            full[k, pl.ds(at, step), :] = total.astype(BF16)

        for j in range(quads):
            if k or j:
                third(k, j).start()
    kept = pltpu.make_async_copy(
        full.at[0, pl.ds(pl.multiple_of(q * quarter_rows, 16), quarter_rows)],
        out.at[q * groups + z],
        own_sem.at[1],
    )
    kept.start()

    def third_in(k, j):
        source = lax.rem(q + quads - j, quads) * groups + lax.rem(z + groups - k, groups)
        return remote(
            full.at[k, pl.ds(0, quarter_rows)], out.at[source],
            sends3, recvs3, k * quads + j, seat(k, j),
        )

    def fourth_in(k):
        return remote(
            grad.at[:, pl.ds(0, piece)], pieces.at[lax.rem(z + groups - k, groups)],
            sends4, recvs4, k, seat(k, 0),
        )

    own_grad.wait()
    for k in range(1, groups):
        fourth(k).wait_send()
        fourth_in(k).wait_recv()
    for k in order:
        first(k, 0).wait_send()
        first(k, 1).wait_send()
        second(k).wait_send()
    for k, j in others:
        third(k, j).wait_send()
        third_in(k, j).wait_recv()
    kept.wait()


def return_rows(part, grad, quads, groups):
    tokens, width = grad.shape
    piece = width // groups
    rows = part.shape[0] // SHARDS
    dma = pltpu.SemaphoreType.DMA
    return pl.pallas_call(
        functools.partial(return_kernel, quads, groups),
        out_shape=(
            jax.ShapeDtypeStruct((quads * groups, rows // quads, piece), BF16),
            jax.ShapeDtypeStruct((groups, tokens, piece), BF16),
        ),
        in_specs=[pl.BlockSpec(memory_space=pltpu.VMEM)] * 2,
        out_specs=[pl.BlockSpec(memory_space=pltpu.VMEM)] * 2,
        scratch_shapes=[
            pltpu.VMEM((2, groups, rows, piece), BF16),
            pltpu.VMEM((groups, rows, piece), BF16),
            pltpu.VMEM((groups, rows, piece), BF16),
            pltpu.VMEM((groups, rows, piece), BF16),
            dma((2,)),
            dma((2 * groups,)),
            dma((2 * groups,)),
            dma((groups,)),
            dma((groups,)),
            dma((groups * quads,)),
            dma((groups * quads,)),
            dma((groups,)),
            dma((groups,)),
        ],
        compiler_params=pltpu.CompilerParams(
            collective_id=0, has_side_effects=True, vmem_limit_bytes=40 << 20
        ),
        name="return_rows",
    )(part, grad)


def gather_kernel(quads, emb, out, own_sem, sends, recvs, core_sends, core_recvs):
    q, x, c, z = place()
    tokens = emb.shape[0]
    cut = tokens // 2
    other_core = (q, x, 1 - c, z)
    other_half = (q, 1 - x, c, z)

    def quad(j):
        return (lax.rem(q + j, quads), x, c, z)

    def source(j):
        return lax.rem(q + quads - j, quads)

    def seat(row, half, core):
        return row * SHARDS + half * 2 + core

    greet([other_core, other_half] + [quad(j) for j in range(1, quads)])
    mine = out.at[seat(q, x, c)]
    own = pltpu.make_async_copy(emb, mine, own_sem)
    own.start()
    low, high = pl.ds(0, cut), pl.ds(cut, cut)

    def across(src, dst, index, partner):
        return remote(src, dst, sends, recvs, index, partner)

    def core_pass(block, core_block, index):
        out_copy = remote(block, block, core_sends, core_recvs, index, other_core)
        in_copy = remote(core_block, core_block, core_sends, core_recvs, index, other_core)
        return out_copy, in_copy

    started, arriving = [], []

    def go(copy):
        copy.start()
        started.append(copy)

    def pass_on(row, half, span, index):
        here, there = out.at[seat(row, half, c)], out.at[seat(row, half, 1 - c)]
        if span is not None:
            here, there = here.at[span], there.at[span]
        out_copy, in_copy = core_pass(here, there, index)
        go(out_copy)
        arriving.append(in_copy)

    go(across(emb, mine, 0, other_half))
    for j in range(1, quads):
        go(across(emb, mine, 3 * j, quad(j)))
    go(remote(emb, mine, core_sends, core_recvs, 0, other_core))
    theirs = out.at[seat(q, x, 1 - c)]
    arriving.append(remote(theirs, theirs, core_sends, core_recvs, 0, other_core))

    half_block = out.at[seat(q, 1 - x, c)]
    across(half_block, half_block, 0, other_half).wait_recv()
    for j in range(1, quads):
        go(across(half_block.at[low], half_block.at[low], 3 * j + 1, quad(j)))
    for j in range(1, quads):
        block = out.at[seat(source(j), x, c)]
        across(block, block, 3 * j, quad(j)).wait_recv()
        go(across(block.at[high], block.at[high], 3 * j + 2, other_half))
        pass_on(source(j), x, None, 4 * j)
    pass_on(q, 1 - x, None, 1)
    for j in range(1, quads):
        block = out.at[seat(source(j), 1 - x, c)]
        across(block.at[low], block.at[low], 3 * j + 1, quad(j)).wait_recv()
        pass_on(source(j), 1 - x, low, 4 * j + 1)
        across(block.at[high], block.at[high], 3 * j + 2, other_half).wait_recv()
        pass_on(source(j), 1 - x, high, 4 * j + 2)
    own.wait()
    for copy in started:
        copy.wait_send()
    for copy in arriving:
        copy.wait_recv()


def gather_plane(emb, quads):
    tokens, piece = emb.shape
    dma = pltpu.SemaphoreType.DMA
    return pl.pallas_call(
        functools.partial(gather_kernel, quads),
        out_shape=jax.ShapeDtypeStruct((quads * SHARDS, tokens, piece), BF16),
        in_specs=[pl.BlockSpec(memory_space=pltpu.VMEM)],
        out_specs=pl.BlockSpec(memory_space=pltpu.VMEM),
        scratch_shapes=[
            dma,
            dma((3 * quads,)),
            dma((3 * quads,)),
            dma((4 * quads,)),
            dma((4 * quads,)),
        ],
        compiler_params=pltpu.CompilerParams(
            collective_id=1, has_side_effects=True, vmem_limit_bytes=40 << 20
        ),
        name="gather_plane",
    )(emb)


def on_device(layer_input, out_grad, expert_ids, combine, bucket_ids, w_gate, w_up, w_down):
    groups = lax.axis_size("blk")
    quads = lax.axis_size("quad")
    experts = groups * quads
    tokens, width = layer_input.shape
    capacity = 5 * tokens // (2 * experts)
    piece = width // groups
    while groups * capacity % 16:
        capacity += 1
    total = experts * capacity

    keys = jnp.concatenate([bucket_ids, expert_ids], axis=1)
    all_keys = lax.all_gather(keys, ("quad", "half", "core", "blk"), tiled=True)
    all_buckets = all_keys[:, :NHASH]
    seat = (lax.axis_index("quad") * 2 + lax.axis_index("half")) * 2 + lax.axis_index("core")
    column = lax.dynamic_slice_in_dim(
        all_keys[:, NHASH:], seat * groups * tokens, groups * tokens, 0
    ).reshape(groups, tokens, 2)

    slots = slot_places(expert_ids, quads, groups, capacity)
    number = jnp.arange(total, dtype=jnp.int32)[:, None]
    first = slots[:, 0][None, :] == number
    second = slots[:, 1][None, :] == number
    pick = (first | second).astype(BF16)
    scale = jnp.sum(
        jnp.where(first, combine[:, 0][None, :], 0.0)
        + jnp.where(second, combine[:, 1][None, :], 0.0),
        axis=1,
        keepdims=True,
    )
    send_x = dot(pick, layer_input, 1, 0).astype(BF16)
    send_w = (dot(pick, out_grad, 1, 0) * scale).astype(BF16)
    both = ("quad", "blk")
    rows_x = lax.all_to_all(send_x, both, split_axis=0, concat_axis=0, tiled=True)
    rows_w = lax.all_to_all(send_w, both, split_axis=0, concat_axis=0, tiled=True)
    rows_x = lax.all_gather(rows_x, SHARD, tiled=True)
    rows_w = lax.all_gather(rows_w, SHARD, tiled=True)

    gate_w, up_w, down_w = w_gate[0, 0], w_up[0, 0], w_down[0, 0]
    gate = dot(rows_x, gate_w, 1, 0)
    upper = dot(rows_x, up_w, 1, 0)
    sigma = jax.nn.sigmoid(gate)
    active = gate * sigma
    hidden = (active * upper).astype(BF16)
    d_hidden = dot(rows_w, down_w, 1, 1)
    d_up = (d_hidden * active).astype(BF16)
    d_gate = (d_hidden * upper * sigma * (1.0 + gate * (1.0 - sigma))).astype(BF16)
    part = (dot(d_gate, gate_w, 1, 1) + dot(d_up, up_w, 1, 1)).astype(BF16)
    grad_d = dot(hidden, rows_w, 0, 0).astype(BF16)
    grad_g = dot(rows_x, d_gate, 0, 0).astype(BF16)
    grad_u = dot(rows_x, d_up, 0, 0).astype(BF16)

    back, grad_pieces = return_rows(part, out_grad, quads, groups)
    puts = []
    for z in range(groups):
        places = slot_places(column[z], quads, groups, capacity)
        expert, position = places // capacity, places % capacity
        puts.append((expert * groups + z) * capacity + position)
    puts = jnp.concatenate(puts, axis=0)
    slot_number = jnp.arange(groups * total, dtype=jnp.int32)[None, :]
    put = (puts[:, :1] == slot_number) | (puts[:, 1:] == slot_number)
    moved = dot(put.astype(BF16), back.reshape(groups * total, piece), 1, 0)
    emb = (grad_pieces.reshape(groups * tokens, piece).astype(F32) + moved).astype(BF16)
    emb_all = gather_plane(emb, quads).reshape(-1, piece)

    base = seat * BUCK_DEV
    local = all_buckets - base
    hot = (local[:, :, None] == jnp.arange(BUCK_DEV)[None, None, :]).astype(BF16)
    hot = hot.reshape(all_buckets.shape[0], NHASH * BUCK_DEV)
    ngram = dot(hot, emb_all, 0, 0).reshape(NHASH, BUCK_DEV, piece)
    return grad_g[None, None], grad_u[None, None], grad_d[None, None], ngram


def solution(mesh):
    blocks = mesh.shape["blk"]
    quads = mesh.shape["dp"] // SHARDS
    split = Mesh(mesh.devices.reshape(quads, 2, 2, blocks), ("quad", "half", "core", "blk"))
    dp = ("quad",) + SHARD
    rows = P(dp + ("blk",), None)
    weights = P("blk", dp, None, None)
    return jax.shard_map(
        on_device,
        mesh=split,
        in_specs=(rows,) * 5 + (weights,) * 3,
        out_specs=(weights,) * 3 + (P(None, dp, "blk"),),
        check_vma=False,
    )
```

```python
import functools

import jax
import jax.numpy as jnp
from jax import lax
from jax.experimental import pallas as pl
from jax.experimental.pallas import tpu as pltpu
from jax.sharding import Mesh, PartitionSpec as P

NHASH = 4
SHARDS = 4
BUCK_DEV = 128
F32 = jnp.float32
BF16 = jnp.bfloat16


def dot(a, b, ca, cb):
    return lax.dot_general(a, b, (((ca,), (cb,)), ((), ())), preferred_element_type=F32)


def slot_places(ids, quads, groups, capacity):
    tokens = ids.shape[0]
    expert_count = quads * groups
    dest = (ids % quads) * groups + ids // quads
    hot = (dest[:, :, None] == jnp.arange(expert_count)[None, None, :]).astype(F32)
    per_token = hot.sum(axis=1)
    before = jnp.tril(jnp.ones((tokens, tokens), F32), -1) @ per_token
    position = (hot * before[:, None, :]).sum(axis=2).astype(jnp.int32)
    return dest * capacity + position


MESH = pl.DeviceIdType.MESH
SHARD = ("half", "core")


def place():
    return tuple(lax.axis_index(name) for name in ("quad", "half", "core", "blk"))


def greet(partners):
    barrier = pltpu.get_barrier_semaphore()
    for partner in partners:
        pl.semaphore_signal(barrier, inc=1, device_id=partner, device_id_type=MESH)
    pl.semaphore_wait(barrier, len(partners))


def remote(src, dst, sends, recvs, index, partner):
    return pltpu.make_async_remote_copy(
        src_ref=src,
        dst_ref=dst,
        send_sem=sends.at[index],
        recv_sem=recvs.at[index],
        device_id=partner,
        device_id_type=MESH,
    )


def return_kernel(
    quads, groups, part, grad, out, pieces, near, pair_sum, far, full, own_sem,
    sends1, recvs1, sends2, recvs2, sends3, recvs3, sends4, recvs4,
):
    q, x, c, z = place()
    rows, piece = full.shape[1], full.shape[2]
    quarter_rows = rows // quads
    others = [(k, j) for k in list(range(1, groups)) + [0] for j in range(quads) if k or j]
    order = list(range(1, groups)) + [0]

    def seat(k, j):
        return (lax.rem(q + j, quads), x, c, lax.rem(z + k, groups))

    other_core = (q, x, 1 - c, z)
    other_half = (q, 1 - x, c, z)
    greet([other_core, other_half] + [seat(k, j) for k, j in others])

    def block(k, j, core):
        half = lax.rem(x + 1 + j, 2)
        row = pl.multiple_of((half * 2 + core) * rows, 32)
        col = pl.multiple_of(lax.rem(z + k, groups) * piece, 128)
        return row, col

    def first(k, j):
        row, col = block(k, j, 1 - c)
        return remote(
            part.at[pl.ds(row, rows), pl.ds(col, piece)], near.at[j, k],
            sends1, recvs1, j * groups + k, other_core,
        )

    def second(k):
        return remote(pair_sum.at[k], far.at[k], sends2, recvs2, k, other_half)

    def third(k, j):
        start = pl.multiple_of(lax.rem(q + j, quads) * quarter_rows, 16)
        return remote(
            full.at[k, pl.ds(start, quarter_rows)], out.at[q * groups + z],
            sends3, recvs3, k * quads + j, seat(k, j),
        )

    def fourth(k):
        col = pl.multiple_of(lax.rem(z + k, groups) * piece, 128)
        return remote(
            grad.at[:, pl.ds(col, piece)], pieces.at[z], sends4, recvs4, k, seat(k, 0)
        )

    for j in range(2):
        for k in order:
            first(k, j).start()
    for k in range(1, groups):
        fourth(k).start()
    own_grad = pltpu.make_async_copy(
        grad.at[:, pl.ds(pl.multiple_of(z * piece, 128), piece)], pieces.at[z], own_sem.at[0]
    )
    own_grad.start()

    step = 32
    for k in order:
        first(k, 0).wait_recv()
        row, col = block(k, 0, c)

        @pl.loop(0, rows // step)
        def _(i):
            at = pl.multiple_of(i * step, step)
            mine = part[pl.ds(pl.multiple_of(row + at, step), step), pl.ds(col, piece)]
            theirs = near[0, k, pl.ds(at, step), :]
            pair_sum[k, pl.ds(at, step), :] = (mine.astype(F32) + theirs.astype(F32)).astype(BF16)

        second(k).start()
    for k in order:
        first(k, 1).wait_recv()
        second(k).wait_recv()
        row, col = block(k, 1, c)

        @pl.loop(0, rows // step)
        def _(i):
            at = pl.multiple_of(i * step, step)
            mine = part[pl.ds(pl.multiple_of(row + at, step), step), pl.ds(col, piece)]
            total = mine.astype(F32) + near[1, k, pl.ds(at, step), :].astype(F32)
            total = total + far[k, pl.ds(at, step), :].astype(F32)
            full[k, pl.ds(at, step), :] = total.astype(BF16)

        for j in range(quads):
            if k or j:
                third(k, j).start()
    kept = pltpu.make_async_copy(
        full.at[0, pl.ds(pl.multiple_of(q * quarter_rows, 16), quarter_rows)],
        out.at[q * groups + z],
        own_sem.at[1],
    )
    kept.start()

    def third_in(k, j):
        source = lax.rem(q + quads - j, quads) * groups + lax.rem(z + groups - k, groups)
        return remote(
            full.at[k, pl.ds(0, quarter_rows)], out.at[source],
            sends3, recvs3, k * quads + j, seat(k, j),
        )

    def fourth_in(k):
        return remote(
            grad.at[:, pl.ds(0, piece)], pieces.at[lax.rem(z + groups - k, groups)],
            sends4, recvs4, k, seat(k, 0),
        )

    own_grad.wait()
    for k in range(1, groups):
        fourth(k).wait_send()
        fourth_in(k).wait_recv()
    for k in order:
        first(k, 0).wait_send()
        first(k, 1).wait_send()
        second(k).wait_send()
    for k, j in others:
        third(k, j).wait_send()
        third_in(k, j).wait_recv()
    kept.wait()


def return_rows(part, grad, quads, groups):
    tokens, width = grad.shape
    piece = width // groups
    rows = part.shape[0] // SHARDS
    dma = pltpu.SemaphoreType.DMA
    return pl.pallas_call(
        functools.partial(return_kernel, quads, groups),
        out_shape=(
            jax.ShapeDtypeStruct((quads * groups, rows // quads, piece), BF16),
            jax.ShapeDtypeStruct((groups, tokens, piece), BF16),
        ),
        in_specs=[pl.BlockSpec(memory_space=pltpu.VMEM)] * 2,
        out_specs=[pl.BlockSpec(memory_space=pltpu.VMEM)] * 2,
        scratch_shapes=[
            pltpu.VMEM((2, groups, rows, piece), BF16),
            pltpu.VMEM((groups, rows, piece), BF16),
            pltpu.VMEM((groups, rows, piece), BF16),
            pltpu.VMEM((groups, rows, piece), BF16),
            dma((2,)),
            dma((2 * groups,)),
            dma((2 * groups,)),
            dma((groups,)),
            dma((groups,)),
            dma((groups * quads,)),
            dma((groups * quads,)),
            dma((groups,)),
            dma((groups,)),
        ],
        compiler_params=pltpu.CompilerParams(
            collective_id=0, has_side_effects=True, vmem_limit_bytes=40 << 20
        ),
        name="return_rows",
    )(part, grad)


def gather_kernel(quads, emb, out, own_sem, sends, recvs, core_sends, core_recvs):
    q, x, c, z = place()
    tokens = emb.shape[0]
    cut = tokens // 2
    other_core = (q, x, 1 - c, z)
    other_half = (q, 1 - x, c, z)

    def quad(j):
        return (lax.rem(q + j, quads), x, c, z)

    def source(j):
        return lax.rem(q + quads - j, quads)

    def seat(row, half, core):
        return row * SHARDS + half * 2 + core

    greet([other_core, other_half] + [quad(j) for j in range(1, quads)])
    mine = out.at[seat(q, x, c)]
    own = pltpu.make_async_copy(emb, mine, own_sem)
    own.start()
    low, high = pl.ds(0, cut), pl.ds(cut, cut)

    def across(src, dst, index, partner):
        return remote(src, dst, sends, recvs, index, partner)

    def core_pass(block, core_block, index):
        out_copy = remote(block, block, core_sends, core_recvs, index, other_core)
        in_copy = remote(core_block, core_block, core_sends, core_recvs, index, other_core)
        return out_copy, in_copy

    started, arriving = [], []

    def go(copy):
        copy.start()
        started.append(copy)

    def pass_on(row, half, span, index):
        here, there = out.at[seat(row, half, c)], out.at[seat(row, half, 1 - c)]
        if span is not None:
            here, there = here.at[span], there.at[span]
        out_copy, in_copy = core_pass(here, there, index)
        go(out_copy)
        arriving.append(in_copy)

    go(across(emb, mine, 0, other_half))
    for j in range(1, quads):
        go(across(emb, mine, 3 * j, quad(j)))
    go(remote(emb, mine, core_sends, core_recvs, 0, other_core))
    theirs = out.at[seat(q, x, 1 - c)]
    arriving.append(remote(theirs, theirs, core_sends, core_recvs, 0, other_core))

    half_block = out.at[seat(q, 1 - x, c)]
    across(half_block, half_block, 0, other_half).wait_recv()
    for j in range(1, quads):
        go(across(half_block.at[low], half_block.at[low], 3 * j + 1, quad(j)))
    for j in range(1, quads):
        block = out.at[seat(source(j), x, c)]
        across(block, block, 3 * j, quad(j)).wait_recv()
        go(across(block.at[high], block.at[high], 3 * j + 2, other_half))
        pass_on(source(j), x, None, 4 * j)
    pass_on(q, 1 - x, None, 1)
    for j in range(1, quads):
        block = out.at[seat(source(j), 1 - x, c)]
        across(block.at[low], block.at[low], 3 * j + 1, quad(j)).wait_recv()
        pass_on(source(j), 1 - x, low, 4 * j + 1)
        across(block.at[high], block.at[high], 3 * j + 2, other_half).wait_recv()
        pass_on(source(j), 1 - x, high, 4 * j + 2)
    own.wait()
    for copy in started:
        copy.wait_send()
    for copy in arriving:
        copy.wait_recv()


def gather_plane(emb, quads):
    tokens, piece = emb.shape
    dma = pltpu.SemaphoreType.DMA
    return pl.pallas_call(
        functools.partial(gather_kernel, quads),
        out_shape=jax.ShapeDtypeStruct((quads * SHARDS, tokens, piece), BF16),
        in_specs=[pl.BlockSpec(memory_space=pltpu.VMEM)],
        out_specs=pl.BlockSpec(memory_space=pltpu.VMEM),
        scratch_shapes=[
            dma,
            dma((3 * quads,)),
            dma((3 * quads,)),
            dma((4 * quads,)),
            dma((4 * quads,)),
        ],
        compiler_params=pltpu.CompilerParams(
            collective_id=1, has_side_effects=True, vmem_limit_bytes=40 << 20
        ),
        name="gather_plane",
    )(emb)


def dispatch_kernel(
    quads, groups, send, out, own_sem, sends1, recvs1, sends2, recvs2, sends3, recvs3
):
    q, x, c, z = place()
    count = quads * groups
    near = [0] + sorted(range(1, groups), key=lambda k: min(k, groups - k))
    others = [(k, j) for k in near for j in range(quads) if k or j]
    other_core = (q, x, 1 - c, z)
    other_half = (q, 1 - x, c, z)
    shard = 2 * x + c
    far_shard = 2 * (1 - x) + c

    def seat(k, j):
        return (lax.rem(q + j, quads), x, c, lax.rem(z + k, groups))

    def target(k, j):
        return lax.rem(q + j, quads) * groups + lax.rem(z + k, groups)

    def source(k, j):
        return lax.rem(q + quads - j, quads) * groups + lax.rem(z + groups - k, groups)

    greet([other_core, other_half] + [seat(k, j) for k, j in others])
    started, arriving = [], []

    def go(copy):
        copy.start()
        started.append(copy)

    def to_half(src, k, j):
        go(remote(src, out.at[shard, source(k, j)], sends2, recvs2, k * quads + j, other_half))

    def to_core(src, whose, k, j):
        index = whose * count + k * quads + j
        block = shard if whose == 0 else far_shard
        go(remote(src, out.at[block, source(k, j)], sends3, recvs3, index, other_core))
        theirs = 2 * (x if whose == 0 else 1 - x) + 1 - c
        got = out.at[theirs, source(k, j)]
        arriving.append(remote(got, got, sends3, recvs3, index, other_core))

    def settle(k, j):
        block = out.at[far_shard, source(k, j)]
        remote(block, block, sends2, recvs2, k * quads + j, other_half).wait_recv()
        to_core(block, 1, k, j)

    home = q * groups + z
    mine = send.at[home]
    to_half(mine, 0, 0)
    for k, j in others:
        go(remote(
            send.at[target(k, j)], out.at[shard, home],
            sends1, recvs1, k * quads + j, seat(k, j),
        ))
    to_core(mine, 0, 0, 0)
    own = pltpu.make_async_copy(mine, out.at[shard, home], own_sem)
    own.start()
    pending = [(0, 0)]
    for k, j in others:
        block = out.at[shard, source(k, j)]
        remote(block, block, sends1, recvs1, k * quads + j, seat(k, j)).wait_recv()
        to_half(block, k, j)
        to_core(block, 0, k, j)
        pending.append((k, j))
        if len(pending) > 2:
            settle(*pending.pop(0))
    for k, j in pending:
        settle(k, j)
    own.wait()
    for copy in started:
        copy.wait_send()
    for copy in arriving:
        copy.wait_recv()


def dispatch(send, quads, groups):
    count = quads * groups
    dma = pltpu.SemaphoreType.DMA
    return pl.pallas_call(
        functools.partial(dispatch_kernel, quads, groups),
        out_shape=jax.ShapeDtypeStruct((SHARDS,) + send.shape, BF16),
        in_specs=[pl.BlockSpec(memory_space=pl.ANY)],
        out_specs=pl.BlockSpec(memory_space=pl.ANY),
        scratch_shapes=[dma] + [dma((count,))] * 4 + [dma((2 * count,))] * 2,
        compiler_params=pltpu.CompilerParams(collective_id=2, has_side_effects=True),
        name="dispatch",
    )(send)


def on_device(layer_input, out_grad, expert_ids, combine, bucket_ids, w_gate, w_up, w_down):
    groups = lax.axis_size("blk")
    quads = lax.axis_size("quad")
    experts = groups * quads
    tokens, width = layer_input.shape
    capacity = 5 * tokens // (2 * experts)
    piece = width // groups
    capacity = -(-capacity // 8) * 8
    total = experts * capacity

    keys = jnp.concatenate([bucket_ids, expert_ids], axis=1)
    all_keys = lax.all_gather(keys, ("quad", "half", "core", "blk"), tiled=True)
    all_buckets = all_keys[:, :NHASH]
    seat = (lax.axis_index("quad") * 2 + lax.axis_index("half")) * 2 + lax.axis_index("core")
    column = lax.dynamic_slice_in_dim(
        all_keys[:, NHASH:], seat * groups * tokens, groups * tokens, 0
    ).reshape(groups, tokens, 2)

    slots = slot_places(expert_ids, quads, groups, capacity)
    number = jnp.arange(total, dtype=jnp.int32)[:, None]
    first = slots[:, 0][None, :] == number
    second = slots[:, 1][None, :] == number
    pick = (first | second).astype(BF16)
    scale = jnp.sum(
        jnp.where(first, combine[:, 0][None, :], 0.0)
        + jnp.where(second, combine[:, 1][None, :], 0.0),
        axis=1,
        keepdims=True,
    )
    send_x = dot(pick, layer_input, 1, 0).astype(BF16)
    send_w = (dot(pick, out_grad, 1, 0) * scale).astype(BF16)
    chunk = (experts, capacity, width)
    send = jnp.concatenate([send_x.reshape(chunk), send_w.reshape(chunk)], axis=1)
    routed = dispatch(send, quads, groups)
    rows_x = routed[:, :, :capacity].reshape(SHARDS * total, width)
    rows_w = routed[:, :, capacity:].reshape(SHARDS * total, width)

    gate_w, up_w, down_w = w_gate[0, 0], w_up[0, 0], w_down[0, 0]
    gate = dot(rows_x, gate_w, 1, 0)
    upper = dot(rows_x, up_w, 1, 0)
    sigma = jax.nn.sigmoid(gate)
    active = gate * sigma
    hidden = (active * upper).astype(BF16)
    d_hidden = dot(rows_w, down_w, 1, 1)
    d_up = (d_hidden * active).astype(BF16)
    d_gate = (d_hidden * upper * sigma * (1.0 + gate * (1.0 - sigma))).astype(BF16)
    part = (dot(d_gate, gate_w, 1, 1) + dot(d_up, up_w, 1, 1)).astype(BF16)
    grad_d = dot(hidden, rows_w, 0, 0).astype(BF16)
    grad_g = dot(rows_x, d_gate, 0, 0).astype(BF16)
    grad_u = dot(rows_x, d_up, 0, 0).astype(BF16)

    back, grad_pieces = return_rows(part, out_grad, quads, groups)
    puts = []
    for z in range(groups):
        places = slot_places(column[z], quads, groups, capacity)
        expert, position = places // capacity, places % capacity
        puts.append((expert * groups + z) * capacity + position)
    puts = jnp.concatenate(puts, axis=0)
    slot_number = jnp.arange(groups * total, dtype=jnp.int32)[None, :]
    put = (puts[:, :1] == slot_number) | (puts[:, 1:] == slot_number)
    moved = dot(put.astype(BF16), back.reshape(groups * total, piece), 1, 0)
    emb = (grad_pieces.reshape(groups * tokens, piece).astype(F32) + moved).astype(BF16)
    emb_all = gather_plane(emb, quads).reshape(-1, piece)

    base = seat * BUCK_DEV
    local = all_buckets - base
    hot = (local[:, :, None] == jnp.arange(BUCK_DEV)[None, None, :]).astype(BF16)
    hot = hot.reshape(all_buckets.shape[0], NHASH * BUCK_DEV)
    ngram = dot(hot, emb_all, 0, 0).reshape(NHASH, BUCK_DEV, piece)
    return grad_g[None, None], grad_u[None, None], grad_d[None, None], ngram


def solution(mesh):
    blocks = mesh.shape["blk"]
    quads = mesh.shape["dp"] // SHARDS
    split = Mesh(mesh.devices.reshape(quads, 2, 2, blocks), ("quad", "half", "core", "blk"))
    dp = ("quad",) + SHARD
    rows = P(dp + ("blk",), None)
    weights = P("blk", dp, None, None)
    return jax.shard_map(
        on_device,
        mesh=split,
        in_specs=(rows,) * 5 + (weights,) * 3,
        out_specs=(weights,) * 3 + (P(None, dp, "blk"),),
        check_vma=False,
    )
```
